512 devices in a mesh: tm: 32 (over z_hi, x, core), space: 16 (over y, z_lo).
Axes of the slice: x: 4, y: 8, z: 8 (z_hi: 4, z_lo: 2; z = z_hi * 2 + z_lo), core: 2. Of those that a mesh axis runs over, the one named last changes fastest.
Arguments:
- incoming_features: bfloat16 [32, 256, 2048], P('tm', 'space'), may hold values from -6 to 6
- frame_noise_grades: int32 [32], replicated, may hold values from 0 to 999
- noise_affine_lookup: bfloat16 [1000, 4, 2048], P(None, None, ('tm', 'space')), may hold values from -3 to 3
- plane_projection_matrix: bfloat16 [2048, 3, 16, 128], P(None, None, 'space'), may hold values from -0.125 to 0.125
- plane_mixing_matrix: bfloat16 [16, 128, 2048], P('space'), may hold values from -0.125 to 0.125
- clock_projection_matrix: bfloat16 [2048, 3, 16, 128], P(None, None, 'space'), may hold values from -0.125 to 0.125
- logit_stretch_factors: float32 [2, 16], replicated, may hold values from 2 to 32, as said below
Outputs:
- mixed: bfloat16 [32, 256, 2048], P('tm', 'space')
- time_heads: bfloat16 [32, 256, 2048], P('tm', None, 'space')
The draws below stay inside these ranges and needn't reach their ends.
Inputs may be any that keep to these rules, and one draw needn't show every extreme that they name: `logit_stretch_factors`: positive score scales of the heads.
All inputs are finite; a program needn't handle non-finite values.
Results may differ from the reference program's by a relative error of at most 0.04.
Values may be sent and summed in bfloat16 or wider, within the bound.
No kernel may reach another device: no remote copies, remote signals or barrier semaphores. Data moves between devices by JAX's collectives and lax.ppermute only.
A program may use at most 64 MiB of HBM per device.

```python
import math
import jax
import jax.numpy as jnp
from jax import lax

D = 2048
HEADS = 16
ATTN_GROUP_SIZE = 128
LEVELS = 1000
FRAMES = 32
NPOS = 256
N_SPACE = 16


def draw_logit_stretch_factors(key, part):
    key = jax.random.fold_in(key, 7)
    gentle = jnp.exp(jax.random.uniform(key, (2, HEADS), jnp.float32, math.log(2.0), math.log(16.0)))
    return gentle.astype(jnp.float32)


def with_ends(array, key, smallest, largest):
    shape = array.shape
    spot = [jax.random.randint(jax.random.fold_in(key, axis), (), 0, shape[axis]) for axis in range(len(shape))]
    array = array.at[tuple(spot)].set(smallest)
    longest = shape.index(max(shape))
    spot[longest] = (spot[longest] + 1) % shape[longest]
    return array.at[tuple(spot)].set(largest)


def steps_of(rng, extent, split, low, largest):
    level, own = 1.0, jax.random.fold_in(rng, 6)
    for position, parts in split:
        heights = jnp.exp(jax.random.uniform(jax.random.fold_in(own, position), (parts,), jnp.float32, low / len(split), largest / len(split)))
        level = level * jnp.repeat(heights, extent[position] // parts).reshape([-1 if axis == position else 1 for axis in range(len(extent))])
    return level


def scatter_about(key, dims, scale, reach, shards=(), held_as=jnp.bfloat16):
    gain = steps_of(key, dims, shards, -0.22, 0.18) if shards else 1.0
    result = jax.random.normal(key, dims, jnp.float32) * scale * gain
    return jnp.minimum(jnp.maximum(result, -reach), reach).astype(held_as)


def setup_inputs(seed: int = 0) -> dict:
    key_of = jax.random.split(jax.random.key(seed), 8)
    return {
        "incoming_features": scatter_about(key_of[0], (FRAMES, NPOS, D), 1.0, 6.0, ((0, 32), (1, 16))),
        "frame_noise_grades": with_ends(jax.random.randint(key_of[1], (FRAMES,), 0, LEVELS), jax.random.fold_in(key_of[1], 1), 0, LEVELS - 1).astype(jnp.int32),
        "noise_affine_lookup": scatter_about(key_of[2], (LEVELS, 4, D), 0.5, 3.0, ((2, 512),)),
        "plane_projection_matrix": scatter_about(key_of[3], (D, 3, HEADS, ATTN_GROUP_SIZE), D ** -0.5, 0.125, ((2, 16),)),
        "plane_mixing_matrix": scatter_about(key_of[4], (HEADS, ATTN_GROUP_SIZE, D), (HEADS * ATTN_GROUP_SIZE) ** -0.5, 0.125, ((0, 16),)),
        "clock_projection_matrix": scatter_about(key_of[5], (D, 3, HEADS, ATTN_GROUP_SIZE), D ** -0.5, 0.125, ((2, 16),)),
        "logit_stretch_factors": draw_logit_stretch_factors(jax.random.fold_in(key_of[7], 71), 0),
    }


def layer_norm(token_rows):
    centre = token_rows - lax.optimization_barrier(jnp.mean(token_rows, axis=-1, keepdims=True))
    spread = lax.optimization_barrier(jnp.mean(centre * centre, axis=-1, keepdims=True))
    return centre * lax.rsqrt(spread + 1e-05)

def unit_rows(vectors):
    return vectors * lax.rsqrt(lax.optimization_barrier(jnp.mean(vectors * vectors, axis=-1, keepdims=True)) + 1e-06)

def soft_weights(scores):
    top_score = lax.optimization_barrier(jnp.max(scores, axis=-1, keepdims=True))
    expo = jnp.exp(scores - top_score)
    return (expo / lax.optimization_barrier(jnp.sum(expo, axis=-1, keepdims=True))).astype(jnp.bfloat16)

def qkv_rows(token_rows, scale_row, shift_row, weight):
    normed = (layer_norm(token_rows.astype(jnp.float32)) * (1.0 + scale_row) + shift_row).astype(jnp.bfloat16)
    flat = weight.reshape(weight.shape[0], -1)
    projected = jnp.dot(normed, flat, preferred_element_type=jnp.float32)
    projected = projected.reshape((token_rows.shape[0],) + weight.shape[1:])
    queries = unit_rows(projected[:, 0]).astype(jnp.bfloat16)
    keys = unit_rows(projected[:, 1]).astype(jnp.bfloat16)
    values = projected[:, 2].astype(jnp.bfloat16)
    return jnp.stack([queries, keys, values], axis=1)

def attend_space(packed, scales):
    queries = packed[:, 0].astype(jnp.float32)
    keys = packed[:, 1].astype(jnp.float32)
    values = packed[:, 2].astype(jnp.float32)
    scores = jnp.einsum('ihd,jhd->hij', queries, keys) * scales[:, None, None]
    weights = soft_weights(scores)
    return jnp.einsum('hij,jhd->ihd', weights.astype(jnp.float32), values).astype(jnp.bfloat16)

def attend_time(packed, scales):
    queries = packed[:, :, 0].astype(jnp.float32)
    keys = packed[:, :, 1].astype(jnp.float32)
    values = packed[:, :, 2].astype(jnp.float32)
    scores = jnp.einsum('fphd,gphd->phfg', queries, keys) * scales[None, :, None, None]
    frame_count = scores.shape[-1]
    causal = lax.broadcasted_iota(jnp.int32, (frame_count, frame_count), 0) >= lax.broadcasted_iota(jnp.int32, (frame_count, frame_count), 1)
    scores = jnp.where(causal[None, None], scores, -1e+30)
    weights = soft_weights(scores)
    output = jnp.einsum('phfg,gphd->fphd', weights.astype(jnp.float32), values).astype(jnp.bfloat16)
    return output.reshape(output.shape[0], output.shape[1], -1)

def reference(incoming_features, frame_noise_grades, noise_affine_lookup, plane_projection_matrix, plane_mixing_matrix, clock_projection_matrix, logit_stretch_factors):
    modulate = jnp.take(noise_affine_lookup, frame_noise_grades, axis=0).astype(jnp.float32)
    plane_stretch_factors = logit_stretch_factors[0] / ATTN_GROUP_SIZE
    clock_stretch_factors = logit_stretch_factors[1] / ATTN_GROUP_SIZE
    local_attn_groups = HEADS // N_SPACE
    out_groups = plane_mixing_matrix.reshape(N_SPACE, local_attn_groups * ATTN_GROUP_SIZE, D).astype(jnp.float32)

    def one_frame(inputs):
        frame_rows, frame_mod = inputs
        packed = qkv_rows(frame_rows, frame_mod[0], frame_mod[1], plane_projection_matrix)
        attended = attend_space(packed, plane_stretch_factors).reshape(NPOS, N_SPACE, local_attn_groups * ATTN_GROUP_SIZE)
        partials = jnp.einsum('ngk,gkd->gnd', attended.astype(jnp.float32), out_groups)
        rounded = lax.optimization_barrier(partials.astype(jnp.bfloat16))
        branch_sum = lax.optimization_barrier(jnp.sum(rounded.astype(jnp.float32), axis=0))
        mixed_rows = (frame_rows.astype(jnp.float32) + branch_sum).astype(jnp.bfloat16)
        return (mixed_rows, qkv_rows(mixed_rows, frame_mod[2], frame_mod[3], clock_projection_matrix))
    mixed, packed_time = lax.map(one_frame, (incoming_features, modulate))
    time_heads = attend_time(packed_time, clock_stretch_factors)
    return (mixed, time_heads)
```

```python
import functools

import jax
import jax.numpy as jnp
from jax import lax
from jax.experimental import pallas as pl
from jax.experimental.pallas import tpu as pltpu
from jax.sharding import Mesh
from jax.sharding import PartitionSpec as P

TM = ("zh", "x", "core")
VMEM_LIMIT = 48 * 1024 * 1024
BF16 = jnp.bfloat16
F32 = jnp.float32


def iota(shape, dim):
    return lax.broadcasted_iota(jnp.int32, shape, dim)


def dot(a, b, dims=((1,), (0,))):
    return lax.dot_general(a, b, (dims, ((), ())), preferred_element_type=F32)


def call(kernel, out, *args, in_smem=(), flops=0, scratch=()):
    specs = [
        pl.BlockSpec(memory_space=pltpu.SMEM if i in in_smem else pltpu.VMEM) for i in range(len(args))
    ]
    outs = jax.tree.map(lambda _: pl.BlockSpec(memory_space=pltpu.VMEM), out)
    total = sum(a.size * a.dtype.itemsize for a in args)
    return pl.pallas_call(
        kernel,
        out_shape=out,
        in_specs=specs,
        out_specs=outs,
        scratch_shapes=scratch,
        compiler_params=pltpu.CompilerParams(vmem_limit_bytes=VMEM_LIMIT),
        cost_estimate=pl.CostEstimate(flops=flops, bytes_accessed=total, transcendentals=0),
    )(*args)


def pack_kernel(grades_ref, table_ref, x_ref, out_ref):
    levels, frames = table_ref.shape[2], grades_ref.shape[1]
    hot = jnp.where(iota((levels, frames), 0) == grades_ref[...], 1.0, 0.0).astype(BF16)
    base = lax.rem(lax.axis_index("y"), 4) * 16
    placed = jnp.zeros((frames, 128), F32)
    for k in range(4):
        picked = dot(table_ref[k], hot).astype(BF16)
        lane = iota((4, 128), 0) + (base + 4 * k)
        place = jnp.where((iota((4, 128), 1) & 63) == lane, 1.0, 0.0).astype(BF16)
        placed = placed + dot(picked, place, ((0,), (0,)))
    packed = jnp.where(iota((16, 128), 1) < 64, placed[0:16], placed[16:32]).astype(BF16)
    for j in range(8):
        out_ref[j, :, 0:2048] = x_ref[0]
        out_ref[j, :, 2048:2176] = packed


def frame_rows_kernel(gathered_ref, out_ref):
    low, high = (
        sum(gathered_ref[4 * half + i, :, 2048:2176].astype(F32) for i in range(4)) for half in range(2)
    )
    left = iota((16, 128), 1) < 64
    first = jnp.where(left, low, pltpu.roll(high, 64, 1))
    second = jnp.where(left, pltpu.roll(low, 64, 1), high)
    rows = jnp.concatenate([first, second, first, second], axis=0)
    out_ref[...] = rows.astype(BF16)


def modulation(rows_ref):
    values = jnp.concatenate([rows_ref[0:32, :], rows_ref[32:64, :]], axis=1)
    n = iota((256, 256), 1)
    source = ((n >> 2) & 1) * 128 + ((n >> 3) & 7) * 16 + (n >> 6) * 4 + (n & 3)
    permute = jnp.where(iota((256, 256), 0) == source, 1.0, 0.0).astype(BF16)
    ordered = dot(values, permute).astype(BF16)
    own_block = (iota((32, 2048), 1) >> 6) == iota((32, 2048), 0)
    rows = []
    for k in range(4):
        lane = (iota((128, 2048), 1) & 63) + 64 * (k % 2)
        spread = jnp.where(iota((128, 2048), 0) == lane, 1.0, 0.0).astype(BF16)
        part = ordered[:, 128 * (k // 2) : 128 * (k // 2) + 128]
        wide = jnp.where(own_block, dot(part, spread), 0.0)
        rows.append(jnp.sum(wide, axis=0, keepdims=True))
    return rows


def normed_rows(rows, scale, shift):
    v = rows.astype(F32)
    centre = v - jnp.mean(v, axis=-1, keepdims=True)
    spread = jnp.mean(centre * centre, axis=-1, keepdims=True)
    return (centre * lax.rsqrt(spread + 1e-05) * (1.0 + scale) + shift).astype(BF16)


def unit(v):
    return v * lax.rsqrt(jnp.mean(v * v, axis=-1, keepdims=True) + 1e-06)


def plane_project_kernel(gathered_ref, rows_ref, own_ref, other_ref, q_ref, kv_ref, mod_ref, normed_ref):
    rows = modulation(rows_ref)
    for k in range(4):
        mod_ref[k : k + 1, :] = rows[k]
    for j in range(8):
        normed_ref[16 * j : 16 * j + 16, :] = normed_rows(gathered_ref[j, :, 0:2048], rows[0], rows[1])
    normed = normed_ref[...]
    even = lax.axis_index("zl") == 0
    for i in range(3):
        both = dot(normed, jnp.concatenate([own_ref[i], other_ref[i]], axis=1))
        own, other = both[:, 0:128], both[:, 128:256]
        if i < 2:
            own, other = unit(own), unit(other)
        for h in range(2):
            part = jnp.where(even, own, other) if h == 0 else jnp.where(even, other, own)
            if i == 0:
                q_ref[h] = part.astype(BF16)
            else:
                kv_ref[h, :, 128 * (i - 1) : 128 * i] = part.astype(BF16)


def plane_attend_kernel(scale_ref, q_ref, kv_ref, far_ref, own_ref, other_ref, out_ref):
    even = lax.axis_index("zl") == 0
    y = lax.axis_index("y")
    heads = []
    for h in range(2):
        scale = scale_ref[0, 2 * y + h] / 128.0
        keys = jnp.concatenate([kv_ref[h, :, 0:128], far_ref[h, :, 0:128]], axis=0)
        values = jnp.concatenate([kv_ref[h, :, 128:256], far_ref[h, :, 128:256]], axis=0)
        scores = dot(q_ref[h], keys, ((1,), (1,))) * scale
        expo = jnp.exp(scores - jnp.max(scores, axis=-1, keepdims=True))
        weights = (expo / jnp.sum(expo, axis=-1, keepdims=True)).astype(BF16)
        heads.append(dot(weights, values))
    own = jnp.where(even, heads[0], heads[1])
    other = jnp.where(even, heads[1], heads[0])
    attended = jnp.concatenate([own, other], axis=1).astype(BF16)
    mixing = jnp.concatenate([own_ref[0], other_ref[0]], axis=0)
    for c in range(0, 2048, 512):
        part = dot(attended, mixing[:, c : c + 512]).astype(BF16)
        for j in range(8):
            out_ref[j, :, c : c + 512] = part[16 * j : 16 * j + 16]


def mix_kernel(terms_ref, x_ref, mixed_ref, spread_ref):
    total = terms_ref[0].astype(F32)
    for j in range(1, 8):
        total = total + terms_ref[j].astype(F32)
    mixed = (x_ref[0].astype(F32) + total).astype(BF16)
    mixed_ref[0] = mixed
    for j in range(8):
        spread_ref[j] = mixed


def clock_project_kernel(gathered_ref, mod_ref, own_ref, other_ref, out_ref, normed_ref):
    scale, shift = mod_ref[2:3, :], mod_ref[3:4, :]
    for j in range(8):
        normed_ref[16 * j : 16 * j + 16, :] = normed_rows(gathered_ref[j], scale, shift)
    normed = normed_ref[...]
    even = lax.axis_index("zl") == 0
    upper = iota((16, 8, 128), 1) < 4
    for i in range(3):
        both = dot(normed, jnp.concatenate([own_ref[i], other_ref[i]], axis=1))
        own, other = both[:, 0:128], both[:, 128:256]
        if i < 2:
            own, other = unit(own), unit(other)
        first = jnp.where(even, own, other).reshape(16, 8, 128)
        second = jnp.where(even, other, own).reshape(16, 8, 128)
        low = jnp.where(upper, first, pltpu.roll(second, 4, 1))
        high = jnp.where(upper, pltpu.roll(first, 4, 1), second)
        rows = jnp.stack([low, high], axis=1).reshape(256, 128)
        out_ref[:, 128 * i : 128 * i + 128] = rows.astype(BF16)


def frame_of(index):
    return (index & 24) + (index & 3) * 2 + ((index >> 2) & 1)


def clock_attend_kernel(scale_ref, rows_ref, out_ref):
    y = lax.axis_index("y")
    queries, keys, values = rows_ref[:, 0:128], rows_ref[:, 128:256], rows_ref[:, 256:384]
    r, c = iota((256, 256), 0), iota((256, 256), 1)
    seen = ((r & 7) == (c & 7)) & (frame_of(c >> 3) <= frame_of(r >> 3))
    scale = jnp.where(
        (iota((256, 1), 0) & 7) < 4, scale_ref[1, 2 * y] / 128.0, scale_ref[1, 2 * y + 1] / 128.0
    )
    scores = jnp.where(seen, dot(queries, keys, ((1,), (1,))) * scale, -1e30)
    expo = jnp.exp(scores - jnp.max(scores, axis=-1, keepdims=True))
    weights = (expo / jnp.sum(expo, axis=-1, keepdims=True)).astype(BF16)
    moved = dot(weights, values).reshape(8, 2, 2, 8, 128)
    upper = iota((8, 2, 8, 128), 2) < 4
    even, odd = moved[:, :, 0], moved[:, :, 1]
    first = jnp.where(upper, even, pltpu.roll(odd, 4, 2))
    second = jnp.where(upper, pltpu.roll(even, 4, 2), odd)
    out_ref[...] = jnp.stack([first, second], axis=1).reshape(256, 128).astype(BF16)


def body(x, grades, table, plane_weight, mixing, clock_weight, stretch):
    def shape(*dims, dtype=BF16):
        return jax.ShapeDtypeStruct(dims, dtype)

    def trade(value, axes):
        return lax.all_to_all(value, axes, split_axis=0, concat_axis=0, tiled=True)

    swaps = []
    for z in range(8):
        for core in range(2):
            z_to = (z ^ 1) if core == 0 else (z + 1 if z % 2 else z - 1) % 8
            swaps.append(((z // 2 * 2 + core) * 2 + z % 2, (z_to // 2 * 2 + core) * 2 + z_to % 2))

    def other_head(weight):
        return lax.ppermute(weight, ("zh", "core", "zl"), swaps)

    plane_weight = jnp.transpose(plane_weight, (1, 2, 0, 3)).reshape(3, 2048, 128)
    clock_weight = jnp.transpose(clock_weight, (1, 2, 0, 3)).reshape(3, 2048, 128)
    far_plane = other_head(plane_weight)

    packed = call(
        pack_kernel, shape(8, 16, 2176), grades.reshape(1, -1), jnp.transpose(table, (1, 2, 0)), x
    )
    gathered = trade(packed, "y")
    own_rows = call(frame_rows_kernel, shape(64, 128), gathered)
    mixing, own_rows = lax.optimization_barrier((mixing, own_rows))
    far_mixing = other_head(mixing)
    rows = trade(own_rows, ("zl",) + TM)
    queries, kv, mod = call(
        plane_project_kernel,
        (shape(2, 128, 128), shape(2, 128, 256), shape(8, 2048, dtype=F32)),
        gathered,
        rows,
        plane_weight,
        far_plane,
        flops=2 * 128 * 2048 * 768,
        scratch=[pltpu.VMEM((128, 2048), BF16)],
    )
    terms = call(
        plane_attend_kernel,
        shape(8, 16, 2048),
        stretch,
        queries,
        kv,
        lax.ppermute(kv, "zl", [(0, 1), (1, 0)]),
        mixing,
        far_mixing,
        in_smem=(0,),
        flops=2 * 128 * 2048 * 256,
    )
    clock_weight, terms = lax.optimization_barrier((clock_weight, terms))
    far_clock = other_head(clock_weight)
    mixed, spread = call(mix_kernel, (shape(1, 16, 2048), shape(8, 16, 2048)), trade(terms, "y"), x)
    clock_rows = call(
        clock_project_kernel,
        shape(256, 384),
        trade(spread, "y"),
        mod,
        clock_weight,
        far_clock,
        flops=2 * 128 * 2048 * 768,
        scratch=[pltpu.VMEM((128, 2048), BF16)],
    )
    by_position = trade(clock_rows, ("zh", "core", "x"))
    moved = call(clock_attend_kernel, shape(256, 128), stretch, by_position, in_smem=(0,))
    heads = trade(moved, ("zh", "core", "zl", "x"))
    return mixed, heads.reshape(1, 256, 128)


def solution(mesh):
    named = Mesh(mesh.devices.reshape(4, 4, 2, 8, 2), ("zh", "x", "core", "y", "zl"))
    space = ("y", "zl")
    return jax.shard_map(
        body,
        mesh=named,
        in_specs=(
            P(TM, space, None),
            P(),
            P(None, None, TM + space),
            P(None, None, space, None),
            P(space, None, None),
            P(None, None, space, None),
            P(),
        ),
        out_specs=(P(TM, space, None), P(TM, None, space)),
        check_vma=False,
    )
```

```python
import functools

import jax
import jax.numpy as jnp
from jax import lax
from jax.experimental import pallas as pl
from jax.experimental.pallas import tpu as pltpu
from jax.sharding import Mesh
from jax.sharding import PartitionSpec as P

TM = ("zh", "x", "core")
VMEM_LIMIT = 16 * 1024 * 1024
BF16 = jnp.bfloat16
F32 = jnp.float32


def iota(shape, dim):
    return lax.broadcasted_iota(jnp.int32, shape, dim)


def dot(a, b, dims=((1,), (0,))):
    return lax.dot_general(a, b, (dims, ((), ())), preferred_element_type=F32)


def call(kernel, out, *args, in_smem=(), flops=0, scratch=()):
    specs = [
        pl.BlockSpec(memory_space=pltpu.SMEM if i in in_smem else pltpu.VMEM) for i in range(len(args))
    ]
    outs = jax.tree.map(lambda _: pl.BlockSpec(memory_space=pltpu.VMEM), out)
    total = sum(a.size * a.dtype.itemsize for a in args)
    return pl.pallas_call(
        kernel,
        out_shape=out,
        in_specs=specs,
        out_specs=outs,
        scratch_shapes=scratch,
        compiler_params=pltpu.CompilerParams(vmem_limit_bytes=VMEM_LIMIT),
        cost_estimate=pl.CostEstimate(flops=flops, bytes_accessed=total, transcendentals=0),
    )(*args)


def pack_kernel(grades_ref, table_ref, x_ref, out_ref):
    levels, frames = table_ref.shape[2], grades_ref.shape[1]
    hot = jnp.where(iota((levels, frames), 0) == grades_ref[...], 1.0, 0.0).astype(BF16)
    base = lax.rem(lax.axis_index("y"), 4) * 16
    placed = jnp.zeros((frames, 128), F32)
    for k in range(4):
        picked = dot(table_ref[k], hot).astype(BF16)
        lane = iota((4, 128), 0) + (base + 4 * k)
        place = jnp.where((iota((4, 128), 1) & 63) == lane, 1.0, 0.0).astype(BF16)
        placed = placed + dot(picked, place, ((0,), (0,)))
    packed = jnp.where(iota((16, 128), 1) < 64, placed[0:16], placed[16:32]).astype(BF16)
    for j in range(8):
        out_ref[j, :, 0:2048] = x_ref[0]
        out_ref[j, :, 2048:2176] = packed


def frame_rows_kernel(gathered_ref, out_ref):
    low, high = (
        sum(gathered_ref[4 * half + i, :, 2048:2176].astype(F32) for i in range(4)) for half in range(2)
    )
    left = iota((16, 128), 1) < 64
    first = jnp.where(left, low, pltpu.roll(high, 64, 1))
    second = jnp.where(left, pltpu.roll(low, 64, 1), high)
    rows = jnp.concatenate([first, second, first, second], axis=0)
    out_ref[...] = rows.astype(BF16)


def modulation(rows_ref):
    values = jnp.concatenate([rows_ref[0:32, :], rows_ref[32:64, :]], axis=1)
    n = iota((256, 256), 1)
    source = ((n >> 2) & 1) * 128 + ((n >> 3) & 7) * 16 + (n >> 6) * 4 + (n & 3)
    permute = jnp.where(iota((256, 256), 0) == source, 1.0, 0.0).astype(BF16)
    ordered = dot(values, permute).astype(BF16)
    own_block = (iota((32, 2048), 1) >> 6) == iota((32, 2048), 0)
    rows = []
    for k in range(4):
        lane = (iota((128, 2048), 1) & 63) + 64 * (k % 2)
        spread = jnp.where(iota((128, 2048), 0) == lane, 1.0, 0.0).astype(BF16)
        part = ordered[:, 128 * (k // 2) : 128 * (k // 2) + 128]
        wide = jnp.where(own_block, dot(part, spread), 0.0)
        rows.append(jnp.sum(wide, axis=0, keepdims=True))
    return rows


def normed_rows(rows, scale, shift):
    v = rows.astype(F32)
    centre = v - jnp.mean(v, axis=-1, keepdims=True)
    spread = jnp.mean(centre * centre, axis=-1, keepdims=True)
    return (centre * lax.rsqrt(spread + 1e-05) * (1.0 + scale) + shift).astype(BF16)


def unit(v):
    return v * lax.rsqrt(jnp.mean(v * v, axis=-1, keepdims=True) + 1e-06)


def plane_project_kernel(gathered_ref, rows_ref, own_ref, other_ref, q_ref, kv_ref, mod_ref, normed_ref):
    rows = modulation(rows_ref)
    for k in range(4):
        mod_ref[k : k + 1, :] = rows[k]
    for j in range(8):
        normed_ref[16 * j : 16 * j + 16, :] = normed_rows(gathered_ref[j, :, 0:2048], rows[0], rows[1])
    normed = normed_ref[...]
    even = lax.axis_index("zl") == 0
    for i in range(3):
        both = dot(normed, jnp.concatenate([own_ref[i], other_ref[i]], axis=1))
        own, other = both[:, 0:128], both[:, 128:256]
        if i < 2:
            own, other = unit(own), unit(other)
        for h in range(2):
            part = jnp.where(even, own, other) if h == 0 else jnp.where(even, other, own)
            if i == 0:
                q_ref[h] = part.astype(BF16)
            else:
                kv_ref[h, :, 128 * (i - 1) : 128 * i] = part.astype(BF16)


def plane_attend_kernel(scale_ref, q_ref, kv_ref, own_ref, other_ref, out_ref):
    even = lax.axis_index("zl") == 0
    y = lax.axis_index("y")
    heads = []
    for h in range(2):
        scale = scale_ref[0, 2 * y + h] / 128.0
        keys = jnp.concatenate([kv_ref[0, h, :, 0:128], kv_ref[1, h, :, 0:128]], axis=0)
        values = jnp.concatenate([kv_ref[0, h, :, 128:256], kv_ref[1, h, :, 128:256]], axis=0)
        scores = dot(q_ref[h], keys, ((1,), (1,))) * scale
        expo = jnp.exp(scores - jnp.max(scores, axis=-1, keepdims=True))
        weights = (expo / jnp.sum(expo, axis=-1, keepdims=True)).astype(BF16)
        heads.append(dot(weights, values))
    own = jnp.where(even, heads[0], heads[1])
    other = jnp.where(even, heads[1], heads[0])
    attended = jnp.concatenate([own, other], axis=1).astype(BF16)
    mixing = jnp.concatenate([own_ref[0], other_ref[0]], axis=0)
    for c in range(0, 2048, 512):
        part = dot(attended, mixing[:, c : c + 512]).astype(BF16)
        for j in range(8):
            out_ref[j, :, c : c + 512] = part[16 * j : 16 * j + 16]


def mix_kernel(terms_ref, x_ref, mixed_ref, spread_ref):
    total = terms_ref[0].astype(F32)
    for j in range(1, 8):
        total = total + terms_ref[j].astype(F32)
    mixed = (x_ref[0].astype(F32) + total).astype(BF16)
    mixed_ref[0] = mixed
    for j in range(8):
        spread_ref[j] = mixed


def clock_project_kernel(gathered_ref, mod_ref, own_ref, other_ref, out_ref, normed_ref):
    scale, shift = mod_ref[2:3, :], mod_ref[3:4, :]
    for j in range(8):
        normed_ref[16 * j : 16 * j + 16, :] = normed_rows(gathered_ref[j], scale, shift)
    normed = normed_ref[...]
    even = lax.axis_index("zl") == 0
    upper = iota((16, 8, 128), 1) < 4
    for i in range(3):
        both = dot(normed, jnp.concatenate([own_ref[i], other_ref[i]], axis=1))
        own, other = both[:, 0:128], both[:, 128:256]
        if i < 2:
            own, other = unit(own), unit(other)
        first = jnp.where(even, own, other).reshape(16, 8, 128)
        second = jnp.where(even, other, own).reshape(16, 8, 128)
        low = jnp.where(upper, first, pltpu.roll(second, 4, 1))
        high = jnp.where(upper, pltpu.roll(first, 4, 1), second)
        rows = jnp.stack([low, high], axis=1).reshape(256, 128)
        out_ref[:, 128 * i : 128 * i + 128] = rows.astype(BF16)


def frame_of(index):
    return (index & 24) + (index & 3) * 2 + ((index >> 2) & 1)


def clock_attend_kernel(scale_ref, rows_ref, out_ref):
    y = lax.axis_index("y")
    queries, keys, values = rows_ref[:, 0:128], rows_ref[:, 128:256], rows_ref[:, 256:384]
    r, c = iota((256, 256), 0), iota((256, 256), 1)
    seen = ((r & 7) == (c & 7)) & (frame_of(c >> 3) <= frame_of(r >> 3))
    scale = jnp.where(
        (iota((256, 1), 0) & 7) < 4, scale_ref[1, 2 * y] / 128.0, scale_ref[1, 2 * y + 1] / 128.0
    )
    scores = jnp.where(seen, dot(queries, keys, ((1,), (1,))) * scale, -1e30)
    expo = jnp.exp(scores - jnp.max(scores, axis=-1, keepdims=True))
    weights = (expo / jnp.sum(expo, axis=-1, keepdims=True)).astype(BF16)
    moved = dot(weights, values).reshape(8, 2, 2, 8, 128)
    upper = iota((8, 2, 8, 128), 2) < 4
    even, odd = moved[:, :, 0], moved[:, :, 1]
    first = jnp.where(upper, even, pltpu.roll(odd, 4, 2))
    second = jnp.where(upper, pltpu.roll(even, 4, 2), odd)
    out_ref[...] = jnp.stack([first, second], axis=1).reshape(256, 128).astype(BF16)


def body(x, grades, table, plane_weight, mixing, clock_weight, stretch):
    def shape(*dims, dtype=BF16):
        return jax.ShapeDtypeStruct(dims, dtype)

    def trade(value, axes):
        return lax.all_to_all(value, axes, split_axis=0, concat_axis=0, tiled=True)

    swaps = []
    for z in range(8):
        for core in range(2):
            z_to = (z ^ 1) if core == 0 else (z + 1 if z % 2 else z - 1) % 8
            swaps.append(((z // 2 * 2 + core) * 2 + z % 2, (z_to // 2 * 2 + core) * 2 + z_to % 2))

    def other_head(weight):
        return lax.ppermute(weight, ("zh", "core", "zl"), swaps)

    plane_weight = jnp.transpose(plane_weight, (1, 2, 0, 3)).reshape(3, 2048, 128)
    clock_weight = jnp.transpose(clock_weight, (1, 2, 0, 3)).reshape(3, 2048, 128)
    packed = call(
        pack_kernel, shape(8, 16, 2176), grades.reshape(1, -1), jnp.transpose(table, (1, 2, 0)), x
    )
    far_plane = other_head(plane_weight)
    packed, mixing = lax.optimization_barrier((packed, mixing))
    far_mixing = other_head(mixing)
    gathered = trade(packed, "y")
    own_rows = call(frame_rows_kernel, shape(64, 128), gathered)
    rows = trade(own_rows, ("zl",) + TM)
    queries, kv, mod = call(
        plane_project_kernel,
        (shape(2, 128, 128), shape(2, 128, 256), shape(8, 2048, dtype=F32)),
        gathered,
        rows,
        plane_weight,
        far_plane,
        flops=2 * 128 * 2048 * 768,
        scratch=[pltpu.VMEM((128, 2048), BF16)],
    )
    terms = call(
        plane_attend_kernel,
        shape(8, 16, 2048),
        stretch,
        queries,
        lax.all_gather(kv, "zl"),
        mixing,
        far_mixing,
        in_smem=(0,),
        flops=2 * 128 * 2048 * 256,
    )
    clock_weight, terms = lax.optimization_barrier((clock_weight, terms))
    far_clock = other_head(clock_weight)
    mixed, spread = call(mix_kernel, (shape(1, 16, 2048), shape(8, 16, 2048)), trade(terms, "y"), x)
    clock_rows = call(
        clock_project_kernel,
        shape(256, 384),
        trade(spread, "y"),
        mod,
        clock_weight,
        far_clock,
        flops=2 * 128 * 2048 * 768,
        scratch=[pltpu.VMEM((128, 2048), BF16)],
    )
    by_position = trade(clock_rows, ("zh", "core", "x"))
    moved = call(clock_attend_kernel, shape(256, 128), stretch, by_position, in_smem=(0,))
    heads = trade(moved, ("zh", "core", "zl", "x"))
    return mixed, heads.reshape(1, 256, 128)


def solution(mesh):
    named = Mesh(mesh.devices.reshape(4, 4, 2, 8, 2), ("zh", "x", "core", "y", "zl"))
    space = ("y", "zl")
    return jax.shard_map(
        body,
        mesh=named,
        in_specs=(
            P(TM, space, None),
            P(),
            P(None, None, TM + space),
            P(None, None, space, None),
            P(space, None, None),
            P(None, None, space, None),
            P(),
        ),
        out_specs=(P(TM, space, None), P(TM, None, space)),
        check_vma=False,
    )
```

```python
import functools

import jax
import jax.numpy as jnp
from jax import lax
from jax.experimental import pallas as pl
from jax.experimental.pallas import tpu as pltpu
from jax.sharding import Mesh
from jax.sharding import PartitionSpec as P

TM = ("zh", "x", "core")
VMEM_LIMIT = 16 * 1024 * 1024
BF16 = jnp.bfloat16
F32 = jnp.float32


def iota(shape, dim):
    return lax.broadcasted_iota(jnp.int32, shape, dim)


def dot(a, b, dims=((1,), (0,))):
    return lax.dot_general(a, b, (dims, ((), ())), preferred_element_type=F32)


def call(kernel, out, *args, in_smem=(), anywhere=(), flops=0, scratch=()):
    def space(i):
        return pltpu.SMEM if i in in_smem else pl.ANY if i in anywhere else pltpu.VMEM

    specs = [pl.BlockSpec(memory_space=space(i)) for i in range(len(args))]
    outs = jax.tree.map(lambda _: pl.BlockSpec(memory_space=pltpu.VMEM), out)
    total = sum(a.size * a.dtype.itemsize for a in args)
    return pl.pallas_call(
        kernel,
        out_shape=out,
        in_specs=specs,
        out_specs=outs,
        scratch_shapes=scratch,
        compiler_params=pltpu.CompilerParams(vmem_limit_bytes=VMEM_LIMIT),
        cost_estimate=pl.CostEstimate(flops=flops, bytes_accessed=total, transcendentals=0),
    )(*args)


def pack_kernel(grades_ref, table_ref, x_ref, out_ref):
    levels, frames = table_ref.shape[2], grades_ref.shape[1]
    hot = jnp.where(iota((levels, frames), 0) == grades_ref[...], 1.0, 0.0).astype(BF16)
    base = lax.rem(lax.axis_index("y"), 4) * 16
    placed = jnp.zeros((frames, 128), F32)
    for k in range(4):
        picked = dot(table_ref[k], hot).astype(BF16)
        lane = iota((4, 128), 0) + (base + 4 * k)
        place = jnp.where((iota((4, 128), 1) & 63) == lane, 1.0, 0.0).astype(BF16)
        placed = placed + dot(picked, place, ((0,), (0,)))
    packed = jnp.where(iota((16, 128), 1) < 64, placed[0:16], placed[16:32]).astype(BF16)
    for j in range(8):
        out_ref[j, :, 0:2048] = x_ref[0]
        out_ref[j, :, 2048:2176] = packed


def frame_rows_kernel(gathered_ref, out_ref):
    low, high = (
        sum(gathered_ref[4 * half + i, :, 2048:2176].astype(F32) for i in range(4)) for half in range(2)
    )
    left = iota((16, 128), 1) < 64
    first = jnp.where(left, low, pltpu.roll(high, 64, 1))
    second = jnp.where(left, pltpu.roll(low, 64, 1), high)
    rows = jnp.concatenate([first, second, first, second], axis=0)
    out_ref[...] = rows.astype(BF16)


def modulation(rows_ref):
    values = jnp.concatenate([rows_ref[0:32, :], rows_ref[32:64, :]], axis=1)
    n = iota((256, 256), 1)
    source = ((n >> 2) & 1) * 128 + ((n >> 3) & 7) * 16 + (n >> 6) * 4 + (n & 3)
    permute = jnp.where(iota((256, 256), 0) == source, 1.0, 0.0).astype(BF16)
    ordered = dot(values, permute).astype(BF16)
    own_block = (iota((32, 2048), 1) >> 6) == iota((32, 2048), 0)
    rows = []
    for k in range(4):
        lane = (iota((128, 2048), 1) & 63) + 64 * (k % 2)
        spread = jnp.where(iota((128, 2048), 0) == lane, 1.0, 0.0).astype(BF16)
        part = ordered[:, 128 * (k // 2) : 128 * (k // 2) + 128]
        wide = jnp.where(own_block, dot(part, spread), 0.0)
        rows.append(jnp.sum(wide, axis=0, keepdims=True))
    return rows


def normed_rows(rows, scale, shift):
    v = rows.astype(F32)
    centre = v - jnp.mean(v, axis=-1, keepdims=True)
    spread = jnp.mean(centre * centre, axis=-1, keepdims=True)
    return (centre * lax.rsqrt(spread + 1e-05) * (1.0 + scale) + shift).astype(BF16)


def unit(v):
    return v * lax.rsqrt(jnp.mean(v * v, axis=-1, keepdims=True) + 1e-06)


def plane_project_kernel(
    gathered_ref, rows_ref, own_ref, other_ref, other_any, q_ref, kv_ref, mod_ref, normed_ref, last_ref, sem
):
    copy = pltpu.make_async_copy(other_any.at[2], last_ref, sem)
    copy.start()
    rows = modulation(rows_ref)
    for k in range(4):
        mod_ref[k : k + 1, :] = rows[k]
    for j in range(8):
        normed_ref[16 * j : 16 * j + 16, :] = normed_rows(gathered_ref[j, :, 0:2048], rows[0], rows[1])
    normed = normed_ref[...]
    even = lax.axis_index("zl") == 0
    for i in range(3):
        if i == 2:
            copy.wait()
        both = dot(normed, jnp.concatenate([own_ref[i], last_ref[...] if i == 2 else other_ref[i]], axis=1))
        own, other = both[:, 0:128], both[:, 128:256]
        if i < 2:
            own, other = unit(own), unit(other)
        for h in range(2):
            part = jnp.where(even, own, other) if h == 0 else jnp.where(even, other, own)
            if i == 0:
                q_ref[h] = part.astype(BF16)
            else:
                kv_ref[h, :, 128 * (i - 1) : 128 * i] = part.astype(BF16)


def plane_attend_kernel(scale_ref, q_ref, kv_ref, own_ref, other_ref, out_ref):
    even = lax.axis_index("zl") == 0
    y = lax.axis_index("y")
    heads = []
    for h in range(2):
        scale = scale_ref[0, 2 * y + h] / 128.0
        keys = jnp.concatenate([kv_ref[0, h, :, 0:128], kv_ref[1, h, :, 0:128]], axis=0)
        values = jnp.concatenate([kv_ref[0, h, :, 128:256], kv_ref[1, h, :, 128:256]], axis=0)
        scores = dot(q_ref[h], keys, ((1,), (1,))) * scale
        expo = jnp.exp(scores - jnp.max(scores, axis=-1, keepdims=True))
        weights = (expo / jnp.sum(expo, axis=-1, keepdims=True)).astype(BF16)
        heads.append(dot(weights, values))
    own = jnp.where(even, heads[0], heads[1])
    other = jnp.where(even, heads[1], heads[0])
    attended = jnp.concatenate([own, other], axis=1).astype(BF16)
    mixing = jnp.concatenate([own_ref[0], other_ref[0]], axis=0)
    for c in range(0, 2048, 512):
        part = dot(attended, mixing[:, c : c + 512]).astype(BF16)
        for j in range(8):
            out_ref[j, :, c : c + 512] = part[16 * j : 16 * j + 16]


def hold_kernel(weight_ref, out_ref):
    out_ref[...] = weight_ref[...]


def hold(weight):
    block = (2,) + weight.shape[1:]
    return pl.pallas_call(
        hold_kernel,
        grid=(1,),
        out_shape=jax.ShapeDtypeStruct(block, weight.dtype),
        in_specs=[pl.BlockSpec(block, lambda i: (0, 0, 0))],
        out_specs=pl.BlockSpec(block, lambda i: (0, 0, 0)),
        compiler_params=pltpu.CompilerParams(vmem_limit_bytes=VMEM_LIMIT),
        cost_estimate=pl.CostEstimate(flops=0, bytes_accessed=2**22, transcendentals=0),
    )(weight)


def mix_kernel(terms_ref, x_ref, mixed_ref, spread_ref):
    total = terms_ref[0].astype(F32)
    for j in range(1, 8):
        total = total + terms_ref[j].astype(F32)
    mixed = (x_ref[0].astype(F32) + total).astype(BF16)
    mixed_ref[0] = mixed
    for j in range(8):
        spread_ref[j] = mixed


def clock_project_kernel(gathered_ref, mod_ref, own_ref, other_ref, out_ref, normed_ref):
    scale, shift = mod_ref[2:3, :], mod_ref[3:4, :]
    for j in range(8):
        normed_ref[16 * j : 16 * j + 16, :] = normed_rows(gathered_ref[j], scale, shift)
    normed = normed_ref[...]
    even = lax.axis_index("zl") == 0
    upper = iota((16, 8, 128), 1) < 4
    for i in range(3):
        both = dot(normed, jnp.concatenate([own_ref[i], other_ref[i]], axis=1))
        own, other = both[:, 0:128], both[:, 128:256]
        if i < 2:
            own, other = unit(own), unit(other)
        first = jnp.where(even, own, other).reshape(16, 8, 128)
        second = jnp.where(even, other, own).reshape(16, 8, 128)
        low = jnp.where(upper, first, pltpu.roll(second, 4, 1))
        high = jnp.where(upper, pltpu.roll(first, 4, 1), second)
        rows = jnp.stack([low, high], axis=1).reshape(256, 128)
        out_ref[:, 128 * i : 128 * i + 128] = rows.astype(BF16)


def frame_of(index):
    return (index & 24) + (index & 3) * 2 + ((index >> 2) & 1)


def clock_attend_kernel(scale_ref, rows_ref, out_ref):
    y = lax.axis_index("y")
    queries, keys, values = rows_ref[:, 0:128], rows_ref[:, 128:256], rows_ref[:, 256:384]
    r, c = iota((256, 256), 0), iota((256, 256), 1)
    seen = ((r & 7) == (c & 7)) & (frame_of(c >> 3) <= frame_of(r >> 3))
    scale = jnp.where(
        (iota((256, 1), 0) & 7) < 4, scale_ref[1, 2 * y] / 128.0, scale_ref[1, 2 * y + 1] / 128.0
    )
    scores = jnp.where(seen, dot(queries, keys, ((1,), (1,))) * scale, -1e30)
    expo = jnp.exp(scores - jnp.max(scores, axis=-1, keepdims=True))
    weights = (expo / jnp.sum(expo, axis=-1, keepdims=True)).astype(BF16)
    moved = dot(weights, values).reshape(8, 2, 2, 8, 128)
    upper = iota((8, 2, 8, 128), 2) < 4
    even, odd = moved[:, :, 0], moved[:, :, 1]
    first = jnp.where(upper, even, pltpu.roll(odd, 4, 2))
    second = jnp.where(upper, pltpu.roll(even, 4, 2), odd)
    out_ref[...] = jnp.stack([first, second], axis=1).reshape(256, 128).astype(BF16)


def body(x, grades, table, plane_weight, mixing, clock_weight, stretch):
    def shape(*dims, dtype=BF16):
        return jax.ShapeDtypeStruct(dims, dtype)

    def trade(value, axes):
        return lax.all_to_all(value, axes, split_axis=0, concat_axis=0, tiled=True)

    swaps = []
    for z in range(8):
        for core in range(2):
            z_to = (z ^ 1) if core == 0 else (z + 1 if z % 2 else z - 1) % 8
            swaps.append(((z // 2 * 2 + core) * 2 + z % 2, (z_to // 2 * 2 + core) * 2 + z_to % 2))

    project_scratch = [
        pltpu.VMEM((128, 2048), BF16),
        pltpu.VMEM((2048, 128), BF16),
        pltpu.SemaphoreType.DMA,
    ]

    def other_head(weight):
        return lax.ppermute(weight, ("zh", "core", "zl"), swaps)

    plane_weight = jnp.transpose(plane_weight, (1, 2, 0, 3)).reshape(3, 2048, 128)
    clock_weight = jnp.transpose(clock_weight, (1, 2, 0, 3)).reshape(3, 2048, 128)
    packed = call(
        pack_kernel, shape(8, 16, 2176), grades.reshape(1, -1), jnp.transpose(table, (1, 2, 0)), x
    )
    far_plane = other_head(plane_weight)
    packed, mixing = lax.optimization_barrier((packed, mixing))
    far_mixing = other_head(mixing)
    gathered = trade(packed, "y")
    own_rows = call(frame_rows_kernel, shape(64, 128), gathered)
    rows = trade(own_rows, ("zl",) + TM)
    queries, kv, mod = call(
        plane_project_kernel,
        (shape(2, 128, 128), shape(2, 128, 256), shape(8, 2048, dtype=F32)),
        gathered,
        rows,
        plane_weight,
        hold(far_plane),
        far_plane,
        anywhere=(4,),
        flops=2 * 128 * 2048 * 768,
        scratch=project_scratch,
    )
    terms = call(
        plane_attend_kernel,
        shape(8, 16, 2048),
        stretch,
        queries,
        lax.all_gather(kv, "zl"),
        mixing,
        far_mixing,
        in_smem=(0,),
        flops=2 * 128 * 2048 * 256,
    )
    clock_weight, terms = lax.optimization_barrier((clock_weight, terms))
    far_clock = other_head(clock_weight)
    mixed, spread = call(mix_kernel, (shape(1, 16, 2048), shape(8, 16, 2048)), trade(terms, "y"), x)
    clock_rows = call(
        clock_project_kernel,
        shape(256, 384),
        trade(spread, "y"),
        mod,
        clock_weight,
        far_clock,
        flops=2 * 128 * 2048 * 768,
        scratch=[pltpu.VMEM((128, 2048), BF16)],
    )
    by_position = trade(clock_rows, ("zh", "core", "x"))
    moved = call(clock_attend_kernel, shape(256, 128), stretch, by_position, in_smem=(0,))
    heads = trade(moved, ("zh", "core", "zl", "x"))
    return mixed, heads.reshape(1, 256, 128)


def solution(mesh):
    named = Mesh(mesh.devices.reshape(4, 4, 2, 8, 2), ("zh", "x", "core", "y", "zl"))
    space = ("y", "zl")
    return jax.shard_map(
        body,
        mesh=named,
        in_specs=(
            P(TM, space, None),
            P(),
            P(None, None, TM + space),
            P(None, None, space, None),
            P(space, None, None),
            P(None, None, space, None),
            P(),
        ),
        out_specs=(P(TM, space, None), P(TM, None, space)),
        check_vma=False,
    )
```

```python
import functools

import jax
import jax.numpy as jnp
from jax import lax
from jax.experimental import pallas as pl
from jax.experimental.pallas import tpu as pltpu
from jax.sharding import Mesh
from jax.sharding import PartitionSpec as P

TM = ("zh", "x", "core")
VMEM_LIMIT = 16 * 1024 * 1024
BF16 = jnp.bfloat16
F32 = jnp.float32


def iota(shape, dim):
    return lax.broadcasted_iota(jnp.int32, shape, dim)


def dot(a, b, dims=((1,), (0,))):
    return lax.dot_general(a, b, (dims, ((), ())), preferred_element_type=F32)


def call(kernel, out, *args, in_smem=(), anywhere=(), flops=0, scratch=()):
    def space(i):
        return pltpu.SMEM if i in in_smem else pl.ANY if i in anywhere else pltpu.VMEM

    specs = [pl.BlockSpec(memory_space=space(i)) for i in range(len(args))]
    outs = jax.tree.map(lambda _: pl.BlockSpec(memory_space=pltpu.VMEM), out)
    total = sum(a.size * a.dtype.itemsize for a in args)
    return pl.pallas_call(
        kernel,
        out_shape=out,
        in_specs=specs,
        out_specs=outs,
        scratch_shapes=scratch,
        compiler_params=pltpu.CompilerParams(vmem_limit_bytes=VMEM_LIMIT),
        cost_estimate=pl.CostEstimate(flops=flops, bytes_accessed=total, transcendentals=0),
    )(*args)


def pack_kernel(grades_ref, table_ref, x_ref, out_ref):
    levels, frames = table_ref.shape[2], grades_ref.shape[1]
    hot = jnp.where(iota((levels, frames), 0) == grades_ref[...], 1.0, 0.0).astype(BF16)
    base = lax.rem(lax.axis_index("y"), 4) * 16
    placed = jnp.zeros((frames, 128), F32)
    for k in range(4):
        picked = dot(table_ref[k], hot).astype(BF16)
        lane = iota((4, 128), 0) + (base + 4 * k)
        place = jnp.where((iota((4, 128), 1) & 63) == lane, 1.0, 0.0).astype(BF16)
        placed = placed + dot(picked, place, ((0,), (0,)))
    packed = jnp.where(iota((16, 128), 1) < 64, placed[0:16], placed[16:32]).astype(BF16)
    for j in range(8):
        out_ref[j, :, 0:2048] = x_ref[0]
        out_ref[j, :, 2048:2176] = packed


def frame_rows_kernel(gathered_ref, out_ref):
    low, high = (
        sum(gathered_ref[4 * half + i, :, 2048:2176].astype(F32) for i in range(4)) for half in range(2)
    )
    plain = lax.axis_index("core") == 0
    low, high = jnp.where(plain, low, high), jnp.where(plain, high, low)
    left = iota((16, 128), 1) < 64
    first = jnp.where(left, low, pltpu.roll(high, 64, 1))
    second = jnp.where(left, pltpu.roll(low, 64, 1), high)
    rows = jnp.concatenate([first, second, first, second], axis=0)
    out_ref[...] = rows.astype(BF16)


def modulation(rows_ref):
    values = jnp.concatenate([rows_ref[0:32, :], rows_ref[32:64, :]], axis=1)
    n = iota((256, 256), 1)
    source = ((n >> 2) & 1) * 128 + ((n >> 3) & 7) * 16 + (n >> 6) * 4 + (n & 3)
    permute = jnp.where(iota((256, 256), 0) == source, 1.0, 0.0).astype(BF16)
    ordered = dot(values, permute).astype(BF16)
    own_block = (iota((32, 2048), 1) >> 6) == iota((32, 2048), 0)
    rows = []
    for k in range(4):
        lane = (iota((128, 2048), 1) & 63) + 64 * (k % 2)
        spread = jnp.where(iota((128, 2048), 0) == lane, 1.0, 0.0).astype(BF16)
        part = ordered[:, 128 * (k // 2) : 128 * (k // 2) + 128]
        wide = jnp.where(own_block, dot(part, spread), 0.0)
        rows.append(jnp.sum(wide, axis=0, keepdims=True))
    return rows


def normed_rows(rows, scale, shift):
    v = rows.astype(F32)
    centre = v - jnp.mean(v, axis=-1, keepdims=True)
    spread = jnp.mean(centre * centre, axis=-1, keepdims=True)
    return (centre * lax.rsqrt(spread + 1e-05) * (1.0 + scale) + shift).astype(BF16)


def unit(v):
    return v * lax.rsqrt(jnp.mean(v * v, axis=-1, keepdims=True) + 1e-06)


def plane_project_kernel(
    gathered_ref, rows_ref, own_ref, other_ref, other_any, q_ref, kv_ref, mod_ref, normed_ref, last_ref, sem
):
    copy = pltpu.make_async_copy(other_any.at[2], last_ref, sem)
    copy.start()
    rows = modulation(rows_ref)
    for k in range(4):
        mod_ref[k : k + 1, :] = rows[k]
    for j in range(8):
        normed_ref[16 * j : 16 * j + 16, :] = normed_rows(gathered_ref[j, :, 0:2048], rows[0], rows[1])
    normed = normed_ref[...]
    even = lax.axis_index("zl") == 0
    for i in range(3):
        if i == 2:
            copy.wait()
        both = dot(normed, jnp.concatenate([own_ref[i], last_ref[...] if i == 2 else other_ref[i]], axis=1))
        own, other = both[:, 0:128], both[:, 128:256]
        if i < 2:
            own, other = unit(own), unit(other)
        for h in range(2):
            part = jnp.where(even, own, other) if h == 0 else jnp.where(even, other, own)
            if i == 0:
                q_ref[h] = part.astype(BF16)
            else:
                kv_ref[h, :, 128 * (i - 1) : 128 * i] = part.astype(BF16)


def plane_attend_kernel(scale_ref, q_ref, kv_ref, own_ref, other_ref, out_ref):
    even = lax.axis_index("zl") == 0
    y = lax.axis_index("y")
    heads = []
    for h in range(2):
        scale = scale_ref[0, 2 * y + h] / 128.0
        keys = jnp.concatenate([kv_ref[0, h, :, 0:128], kv_ref[1, h, :, 0:128]], axis=0)
        values = jnp.concatenate([kv_ref[0, h, :, 128:256], kv_ref[1, h, :, 128:256]], axis=0)
        scores = dot(q_ref[h], keys, ((1,), (1,))) * scale
        expo = jnp.exp(scores - jnp.max(scores, axis=-1, keepdims=True))
        weights = (expo / jnp.sum(expo, axis=-1, keepdims=True)).astype(BF16)
        heads.append(dot(weights, values))
    own = jnp.where(even, heads[0], heads[1])
    other = jnp.where(even, heads[1], heads[0])
    attended = jnp.concatenate([own, other], axis=1).astype(BF16)
    mixing = jnp.concatenate([own_ref[0], other_ref[0]], axis=0)
    for c in range(0, 2048, 512):
        part = dot(attended, mixing[:, c : c + 512]).astype(BF16)
        for j in range(8):
            out_ref[j, :, c : c + 512] = part[16 * j : 16 * j + 16]


def hold_kernel(weight_ref, out_ref):
    out_ref[...] = weight_ref[...]


def hold(weight):
    block = (2,) + weight.shape[1:]
    return pl.pallas_call(
        hold_kernel,
        grid=(1,),
        out_shape=jax.ShapeDtypeStruct(block, weight.dtype),
        in_specs=[pl.BlockSpec(block, lambda i: (0, 0, 0))],
        out_specs=pl.BlockSpec(block, lambda i: (0, 0, 0)),
        compiler_params=pltpu.CompilerParams(vmem_limit_bytes=VMEM_LIMIT),
        cost_estimate=pl.CostEstimate(flops=0, bytes_accessed=2**22, transcendentals=0),
    )(weight)


def mix_kernel(terms_ref, x_ref, mixed_ref, spread_ref):
    total = terms_ref[0].astype(F32)
    for j in range(1, 8):
        total = total + terms_ref[j].astype(F32)
    mixed = (x_ref[0].astype(F32) + total).astype(BF16)
    mixed_ref[0] = mixed
    for j in range(8):
        spread_ref[j] = mixed


def clock_project_kernel(gathered_ref, mod_ref, own_ref, other_ref, out_ref, normed_ref):
    scale, shift = mod_ref[2:3, :], mod_ref[3:4, :]
    for j in range(8):
        normed_ref[16 * j : 16 * j + 16, :] = normed_rows(gathered_ref[j], scale, shift)
    normed = normed_ref[...]
    even = lax.axis_index("zl") == 0
    plain = lax.axis_index("core") == 0
    upper = iota((16, 8, 128), 1) < 4
    for i in range(3):
        both = dot(normed, jnp.concatenate([own_ref[i], other_ref[i]], axis=1))
        own, other = both[:, 0:128], both[:, 128:256]
        if i < 2:
            own, other = unit(own), unit(other)
        first = jnp.where(even, own, other).reshape(16, 8, 128)
        second = jnp.where(even, other, own).reshape(16, 8, 128)
        low = jnp.where(upper, first, pltpu.roll(second, 4, 1))
        high = jnp.where(upper, pltpu.roll(first, 4, 1), second)
        rows = jnp.stack([low, high], axis=1).reshape(256, 128).astype(BF16)
        halves = rows[0:128], rows[128:256]
        out_ref[0:128, 128 * i : 128 * i + 128] = jnp.where(plain, halves[0], halves[1])
        out_ref[128:256, 128 * i : 128 * i + 128] = jnp.where(plain, halves[1], halves[0])


def frame_of(index):
    return (index & 24) + (index & 3) * 2 + ((index >> 2) & 1)


def clock_attend_kernel(scale_ref, rows_ref, out_ref):
    y = lax.axis_index("y")
    queries, keys, values = rows_ref[:, 0:128], rows_ref[:, 128:256], rows_ref[:, 256:384]
    r, c = iota((256, 256), 0), iota((256, 256), 1)
    seen = ((r & 7) == (c & 7)) & (frame_of(c >> 3) <= frame_of(r >> 3))
    scale = jnp.where(
        (iota((256, 1), 0) & 7) < 4, scale_ref[1, 2 * y] / 128.0, scale_ref[1, 2 * y + 1] / 128.0
    )
    scores = jnp.where(seen, dot(queries, keys, ((1,), (1,))) * scale, -1e30)
    expo = jnp.exp(scores - jnp.max(scores, axis=-1, keepdims=True))
    weights = (expo / jnp.sum(expo, axis=-1, keepdims=True)).astype(BF16)
    moved = dot(weights, values).reshape(8, 2, 2, 8, 128)
    upper = iota((8, 2, 8, 128), 2) < 4
    even, odd = moved[:, :, 0], moved[:, :, 1]
    first = jnp.where(upper, even, pltpu.roll(odd, 4, 2))
    second = jnp.where(upper, pltpu.roll(even, 4, 2), odd)
    out_ref[...] = jnp.stack([first, second], axis=1).reshape(256, 128).astype(BF16)


def body(x, grades, table, plane_weight, mixing, clock_weight, stretch):
    def shape(*dims, dtype=BF16):
        return jax.ShapeDtypeStruct(dims, dtype)

    def trade(value, axes, groups=None):
        return lax.all_to_all(
            value, axes, split_axis=0, concat_axis=0, tiled=True, axis_index_groups=groups
        )

    ring = [list(range(8)), [8 + (y + 4) % 8 for y in range(8)]]

    def trade_ring(value):
        return trade(value, ("core", "y"), ring)

    swaps = []
    for z in range(8):
        for core in range(2):
            z_to = (z ^ 1) if core == 0 else (z + 1 if z % 2 else z - 1) % 8
            swaps.append(((z // 2 * 2 + core) * 2 + z % 2, (z_to // 2 * 2 + core) * 2 + z_to % 2))

    project_scratch = [
        pltpu.VMEM((128, 2048), BF16),
        pltpu.VMEM((2048, 128), BF16),
        pltpu.SemaphoreType.DMA,
    ]

    def other_head(weight):
        return lax.ppermute(weight, ("zh", "core", "zl"), swaps)

    plane_weight = jnp.transpose(plane_weight, (1, 2, 0, 3)).reshape(3, 2048, 128)
    clock_weight = jnp.transpose(clock_weight, (1, 2, 0, 3)).reshape(3, 2048, 128)
    packed = call(
        pack_kernel, shape(8, 16, 2176), grades.reshape(1, -1), jnp.transpose(table, (1, 2, 0)), x
    )
    far_plane = other_head(plane_weight)
    packed, mixing = lax.optimization_barrier((packed, mixing))
    far_mixing = other_head(mixing)
    gathered = trade_ring(packed)
    own_rows = call(frame_rows_kernel, shape(64, 128), gathered)
    rows = trade(own_rows, ("zl",) + TM)
    queries, kv, mod = call(
        plane_project_kernel,
        (shape(2, 128, 128), shape(2, 128, 256), shape(8, 2048, dtype=F32)),
        gathered,
        rows,
        plane_weight,
        hold(far_plane),
        far_plane,
        anywhere=(4,),
        flops=2 * 128 * 2048 * 768,
        scratch=project_scratch,
    )
    terms = call(
        plane_attend_kernel,
        shape(8, 16, 2048),
        stretch,
        queries,
        lax.all_gather(kv, "zl"),
        mixing,
        far_mixing,
        in_smem=(0,),
        flops=2 * 128 * 2048 * 256,
    )
    clock_weight, terms = lax.optimization_barrier((clock_weight, terms))
    far_clock = other_head(clock_weight)
    mixed, spread = call(mix_kernel, (shape(1, 16, 2048), shape(8, 16, 2048)), trade_ring(terms), x)
    clock_rows = call(
        clock_project_kernel,
        shape(256, 384),
        trade_ring(spread),
        mod,
        clock_weight,
        far_clock,
        flops=2 * 128 * 2048 * 768,
        scratch=[pltpu.VMEM((128, 2048), BF16)],
    )
    by_position = trade(clock_rows, ("zh", "core", "x"))
    moved = call(clock_attend_kernel, shape(256, 128), stretch, by_position, in_smem=(0,))
    heads = trade(moved, ("zh", "core", "zl", "x"))
    return mixed, heads.reshape(1, 256, 128)


def solution(mesh):
    named = Mesh(mesh.devices.reshape(4, 4, 2, 8, 2), ("zh", "x", "core", "y", "zl"))
    space = ("y", "zl")
    return jax.shard_map(
        body,
        mesh=named,
        in_specs=(
            P(TM, space, None),
            P(),
            P(None, None, TM + space),
            P(None, None, space, None),
            P(space, None, None),
            P(None, None, space, None),
            P(),
        ),
        out_specs=(P(TM, space, None), P(TM, None, space)),
        check_vma=False,
    )
```

```python
import functools

import jax
import jax.numpy as jnp
from jax import lax
from jax.experimental import pallas as pl
from jax.experimental.pallas import tpu as pltpu
from jax.sharding import Mesh
from jax.sharding import PartitionSpec as P

TM = ("zh", "x", "core")
VMEM_LIMIT = 16 * 1024 * 1024
BF16 = jnp.bfloat16
F32 = jnp.float32


def iota(shape, dim):
    return lax.broadcasted_iota(jnp.int32, shape, dim)


def dot(a, b, dims=((1,), (0,))):
    return lax.dot_general(a, b, (dims, ((), ())), preferred_element_type=F32)


def call(kernel, out, *args, in_smem=(), anywhere=(), flops=0, scratch=()):
    def space(i):
        return pltpu.SMEM if i in in_smem else pl.ANY if i in anywhere else pltpu.VMEM

    specs = [pl.BlockSpec(memory_space=space(i)) for i in range(len(args))]
    outs = jax.tree.map(lambda _: pl.BlockSpec(memory_space=pltpu.VMEM), out)
    total = sum(a.size * a.dtype.itemsize for a in args)
    return pl.pallas_call(
        kernel,
        out_shape=out,
        in_specs=specs,
        out_specs=outs,
        scratch_shapes=scratch,
        compiler_params=pltpu.CompilerParams(vmem_limit_bytes=VMEM_LIMIT),
        cost_estimate=pl.CostEstimate(flops=flops, bytes_accessed=total, transcendentals=0),
    )(*args)


def pack_kernel(grades_ref, table_ref, x_ref, out_ref):
    levels, frames = table_ref.shape[2], grades_ref.shape[1]
    hot = jnp.where(iota((levels, frames), 0) == grades_ref[...], 1.0, 0.0).astype(BF16)
    base = lax.rem(lax.axis_index("y"), 4) * 16
    placed = jnp.zeros((frames, 128), F32)
    for k in range(4):
        picked = dot(table_ref[k], hot).astype(BF16)
        lane = iota((4, 128), 0) + (base + 4 * k)
        place = jnp.where((iota((4, 128), 1) & 63) == lane, 1.0, 0.0).astype(BF16)
        placed = placed + dot(picked, place, ((0,), (0,)))
    packed = jnp.where(iota((16, 128), 1) < 64, placed[0:16], placed[16:32]).astype(BF16)
    for j in range(8):
        out_ref[j, :, 0:2048] = x_ref[0]
        out_ref[j, :, 2048:2176] = packed


def frame_rows_kernel(gathered_ref, out_ref):
    low, high = (
        sum(gathered_ref[4 * half + i, :, 2048:2176].astype(F32) for i in range(4)) for half in range(2)
    )
    plain = lax.axis_index("core") == 0
    low, high = jnp.where(plain, low, high), jnp.where(plain, high, low)
    left = iota((16, 128), 1) < 64
    first = jnp.where(left, low, pltpu.roll(high, 64, 1))
    second = jnp.where(left, pltpu.roll(low, 64, 1), high)
    rows = jnp.concatenate([first, second, first, second], axis=0)
    out_ref[...] = rows.astype(BF16)


def modulation(rows_ref):
    values = jnp.concatenate([rows_ref[0:32, :], rows_ref[32:64, :]], axis=1)
    n = iota((256, 256), 1)
    source = ((n >> 2) & 1) * 128 + ((n >> 3) & 7) * 16 + (n >> 6) * 4 + (n & 3)
    permute = jnp.where(iota((256, 256), 0) == source, 1.0, 0.0).astype(BF16)
    ordered = dot(values, permute).astype(BF16)
    own_block = (iota((32, 2048), 1) >> 6) == iota((32, 2048), 0)
    rows = []
    for k in range(4):
        lane = (iota((128, 2048), 1) & 63) + 64 * (k % 2)
        spread = jnp.where(iota((128, 2048), 0) == lane, 1.0, 0.0).astype(BF16)
        part = ordered[:, 128 * (k // 2) : 128 * (k // 2) + 128]
        wide = jnp.where(own_block, dot(part, spread), 0.0)
        rows.append(jnp.sum(wide, axis=0, keepdims=True))
    return rows


def normed_rows(rows, scale, shift):
    v = rows.astype(F32)
    centre = v - jnp.mean(v, axis=-1, keepdims=True)
    spread = jnp.mean(centre * centre, axis=-1, keepdims=True)
    return (centre * lax.rsqrt(spread + 1e-05) * (1.0 + scale) + shift).astype(BF16)


def unit(v):
    return v * lax.rsqrt(jnp.mean(v * v, axis=-1, keepdims=True) + 1e-06)


def plane_project_kernel(
    gathered_ref, rows_ref, own_ref, other_ref, other_any, q_ref, kv_ref, mod_ref, normed_ref, last_ref, sem
):
    copy = pltpu.make_async_copy(other_any.at[2], last_ref, sem)
    copy.start()
    rows = modulation(rows_ref)
    for k in range(4):
        mod_ref[k : k + 1, :] = rows[k]
    for j in range(8):
        normed_ref[16 * j : 16 * j + 16, :] = normed_rows(gathered_ref[j, :, 0:2048], rows[0], rows[1])
    normed = normed_ref[...]
    even = lax.axis_index("zl") == 0
    for i in range(3):
        if i == 2:
            copy.wait()
        both = dot(normed, jnp.concatenate([own_ref[i], last_ref[...] if i == 2 else other_ref[i]], axis=1))
        own, other = both[:, 0:128], both[:, 128:256]
        if i < 2:
            own, other = unit(own), unit(other)
        for h in range(2):
            part = jnp.where(even, own, other) if h == 0 else jnp.where(even, other, own)
            if i == 0:
                q_ref[h] = part.astype(BF16)
            else:
                kv_ref[h, :, 128 * (i - 1) : 128 * i] = part.astype(BF16)


def plane_attend_kernel(scale_ref, q_ref, kv_ref, own_ref, other_ref, out_ref):
    even = lax.axis_index("zl") == 0
    y = lax.axis_index("y")
    heads = []
    for h in range(2):
        scale = scale_ref[0, 2 * y + h] / 128.0
        keys = jnp.concatenate([kv_ref[0, h, :, 0:128], kv_ref[1, h, :, 0:128]], axis=0)
        values = jnp.concatenate([kv_ref[0, h, :, 128:256], kv_ref[1, h, :, 128:256]], axis=0)
        scores = dot(q_ref[h], keys, ((1,), (1,))) * scale
        expo = jnp.exp(scores - jnp.max(scores, axis=-1, keepdims=True))
        weights = (expo / jnp.sum(expo, axis=-1, keepdims=True)).astype(BF16)
        heads.append(dot(weights, values))
    own = jnp.where(even, heads[0], heads[1])
    other = jnp.where(even, heads[1], heads[0])
    attended = jnp.concatenate([own, other], axis=1).astype(BF16)
    mixing = jnp.concatenate([own_ref[0], other_ref[0]], axis=0)
    for c in range(0, 2048, 512):
        part = dot(attended, mixing[:, c : c + 512]).astype(BF16)
        for j in range(8):
            out_ref[j, :, c : c + 512] = part[16 * j : 16 * j + 16]


def hold_kernel(weight_ref, out_ref):
    out_ref[...] = weight_ref[...]


def hold(weight):
    block = (2,) + weight.shape[1:]
    return pl.pallas_call(
        hold_kernel,
        grid=(1,),
        out_shape=jax.ShapeDtypeStruct(block, weight.dtype),
        in_specs=[pl.BlockSpec(block, lambda i: (0, 0, 0))],
        out_specs=pl.BlockSpec(block, lambda i: (0, 0, 0)),
        compiler_params=pltpu.CompilerParams(vmem_limit_bytes=VMEM_LIMIT),
        cost_estimate=pl.CostEstimate(flops=0, bytes_accessed=2**22, transcendentals=0),
    )(weight)


def mix_kernel(terms_ref, x_ref, mixed_ref, spread_ref):
    total = terms_ref[0].astype(F32)
    for j in range(1, 8):
        total = total + terms_ref[j].astype(F32)
    mixed = (x_ref[0].astype(F32) + total).astype(BF16)
    mixed_ref[0] = mixed
    for j in range(8):
        spread_ref[j] = mixed


def clock_project_kernel(gathered_ref, mod_ref, own_ref, other_ref, out_ref, normed_ref):
    scale, shift = mod_ref[2:3, :], mod_ref[3:4, :]
    for j in range(8):
        normed_ref[16 * j : 16 * j + 16, :] = normed_rows(gathered_ref[j], scale, shift)
    normed = normed_ref[...]
    even = lax.axis_index("zl") == 0
    plain = lax.axis_index("core") == 0
    upper = iota((16, 8, 128), 1) < 4
    for i in range(3):
        both = dot(normed, jnp.concatenate([own_ref[i], other_ref[i]], axis=1))
        own, other = both[:, 0:128], both[:, 128:256]
        if i < 2:
            own, other = unit(own), unit(other)
        first = jnp.where(even, own, other).reshape(16, 8, 128)
        second = jnp.where(even, other, own).reshape(16, 8, 128)
        low = jnp.where(upper, first, pltpu.roll(second, 4, 1))
        high = jnp.where(upper, pltpu.roll(first, 4, 1), second)
        rows = jnp.stack([low, high], axis=1).reshape(256, 128).astype(BF16)
        halves = rows[0:128], rows[128:256]
        out_ref[0:128, 128 * i : 128 * i + 128] = jnp.where(plain, halves[0], halves[1])
        out_ref[128:256, 128 * i : 128 * i + 128] = jnp.where(plain, halves[1], halves[0])


def frame_of(index):
    return (index & 24) + (index & 3) * 2 + ((index >> 2) & 1)


def clock_attend_kernel(scale_ref, rows_ref, out_ref):
    y = lax.axis_index("y")
    queries, keys, values = rows_ref[:, 0:128], rows_ref[:, 128:256], rows_ref[:, 256:384]
    r, c = iota((256, 256), 0), iota((256, 256), 1)
    seen = ((r & 7) == (c & 7)) & (frame_of(c >> 3) <= frame_of(r >> 3))
    scale = jnp.where(
        (iota((256, 1), 0) & 7) < 4, scale_ref[1, 2 * y] / 128.0, scale_ref[1, 2 * y + 1] / 128.0
    )
    scores = jnp.where(seen, dot(queries, keys, ((1,), (1,))) * scale, -1e30)
    expo = jnp.exp(scores - jnp.max(scores, axis=-1, keepdims=True))
    weights = (expo / jnp.sum(expo, axis=-1, keepdims=True)).astype(BF16)
    moved = dot(weights, values).reshape(8, 2, 2, 8, 128)
    upper = iota((8, 2, 8, 128), 2) < 4
    even, odd = moved[:, :, 0], moved[:, :, 1]
    first = jnp.where(upper, even, pltpu.roll(odd, 4, 2))
    second = jnp.where(upper, pltpu.roll(even, 4, 2), odd)
    out_ref[...] = jnp.stack([first, second], axis=1).reshape(256, 128).astype(BF16)


def body(x, grades, table, plane_weight, mixing, clock_weight, stretch):
    def shape(*dims, dtype=BF16):
        return jax.ShapeDtypeStruct(dims, dtype)

    def trade(value, axes, groups=None):
        return lax.all_to_all(
            value, axes, split_axis=0, concat_axis=0, tiled=True, axis_index_groups=groups
        )

    ring = [list(range(8)), [8 + (y + 4) % 8 for y in range(8)]]

    def trade_ring(value):
        return trade(value, ("core", "y"), ring)

    swaps = []
    for z in range(8):
        for core in range(2):
            z_to = (z ^ 1) if core == 0 else (z + 1 if z % 2 else z - 1) % 8
            swaps.append(((z // 2 * 2 + core) * 2 + z % 2, (z_to // 2 * 2 + core) * 2 + z_to % 2))

    project_scratch = [
        pltpu.VMEM((128, 2048), BF16),
        pltpu.VMEM((2048, 128), BF16),
        pltpu.SemaphoreType.DMA,
    ]

    def other_head(weight):
        return lax.ppermute(weight, ("zh", "core", "zl"), swaps)

    plane_weight = jnp.transpose(plane_weight, (1, 2, 0, 3)).reshape(3, 2048, 128)
    clock_weight = jnp.transpose(clock_weight, (1, 2, 0, 3)).reshape(3, 2048, 128)
    packed = call(
        pack_kernel, shape(8, 16, 2176), grades.reshape(1, -1), jnp.transpose(table, (1, 2, 0)), x
    )
    far_plane = other_head(plane_weight)
    packed, mixing = lax.optimization_barrier((packed, mixing))
    far_mixing = other_head(mixing)
    gathered = trade_ring(packed)
    own_rows = call(frame_rows_kernel, shape(64, 128), gathered)
    rows = trade(own_rows, ("zl",) + TM)
    queries, kv, mod = call(
        plane_project_kernel,
        (shape(2, 128, 128), shape(2, 128, 256), shape(8, 2048, dtype=F32)),
        gathered,
        rows,
        plane_weight,
        hold(far_plane),
        far_plane,
        anywhere=(4,),
        flops=2 * 128 * 2048 * 768,
        scratch=project_scratch,
    )
    terms = call(
        plane_attend_kernel,
        shape(8, 16, 2048),
        stretch,
        queries,
        lax.all_gather(kv, "zl"),
        mixing,
        far_mixing,
        in_smem=(0,),
        flops=2 * 128 * 2048 * 256,
    )
    clock_weight, terms = lax.optimization_barrier((clock_weight, terms))
    far_clock = other_head(clock_weight)
    mixed, spread = call(mix_kernel, (shape(1, 16, 2048), shape(8, 16, 2048)), trade_ring(terms), x)
    spread, far_clock = lax.optimization_barrier((spread, far_clock))
    clock_rows = call(
        clock_project_kernel,
        shape(256, 384),
        trade_ring(spread),
        mod,
        clock_weight,
        far_clock,
        flops=2 * 128 * 2048 * 768,
        scratch=[pltpu.VMEM((128, 2048), BF16)],
    )
    by_position = trade(clock_rows, ("zh", "core", "x"))
    moved = call(clock_attend_kernel, shape(256, 128), stretch, by_position, in_smem=(0,))
    heads = trade(moved, ("zh", "core", "zl", "x"))
    return mixed, heads.reshape(1, 256, 128)


def solution(mesh):
    named = Mesh(mesh.devices.reshape(4, 4, 2, 8, 2), ("zh", "x", "core", "y", "zl"))
    space = ("y", "zl")
    return jax.shard_map(
        body,
        mesh=named,
        in_specs=(
            P(TM, space, None),
            P(),
            P(None, None, TM + space),
            P(None, None, space, None),
            P(space, None, None),
            P(None, None, space, None),
            P(),
        ),
        out_specs=(P(TM, space, None), P(TM, None, space)),
        check_vma=False,
    )
```

```python
import functools

import jax
import jax.numpy as jnp
from jax import lax
from jax.experimental import pallas as pl
from jax.experimental.pallas import tpu as pltpu
from jax.sharding import Mesh
from jax.sharding import PartitionSpec as P

TM = ("zh", "x", "core")
VMEM_LIMIT = 16 * 1024 * 1024
BF16 = jnp.bfloat16
F32 = jnp.float32


def iota(shape, dim):
    return lax.broadcasted_iota(jnp.int32, shape, dim)


def dot(a, b, dims=((1,), (0,))):
    return lax.dot_general(a, b, (dims, ((), ())), preferred_element_type=F32)


def call(kernel, out, *args, in_smem=(), anywhere=(), flops=0, scratch=()):
    def space(i):
        return pltpu.SMEM if i in in_smem else pl.ANY if i in anywhere else pltpu.VMEM

    specs = [pl.BlockSpec(memory_space=space(i)) for i in range(len(args))]
    outs = jax.tree.map(lambda _: pl.BlockSpec(memory_space=pltpu.VMEM), out)
    total = sum(a.size * a.dtype.itemsize for a in args)
    return pl.pallas_call(
        kernel,
        out_shape=out,
        in_specs=specs,
        out_specs=outs,
        scratch_shapes=scratch,
        compiler_params=pltpu.CompilerParams(vmem_limit_bytes=VMEM_LIMIT),
        cost_estimate=pl.CostEstimate(flops=flops, bytes_accessed=total, transcendentals=0),
    )(*args)


def pack_kernel(grades_ref, table_ref, x_ref, out_ref):
    levels, frames = table_ref.shape[2], grades_ref.shape[1]
    hot = jnp.where(iota((levels, frames), 0) == grades_ref[...], 1.0, 0.0).astype(BF16)
    base = lax.rem(lax.axis_index("y"), 4) * 16
    placed = jnp.zeros((frames, 128), F32)
    for k in range(4):
        picked = dot(table_ref[k], hot).astype(BF16)
        lane = iota((4, 128), 0) + (base + 4 * k)
        place = jnp.where((iota((4, 128), 1) & 63) == lane, 1.0, 0.0).astype(BF16)
        placed = placed + dot(picked, place, ((0,), (0,)))
    packed = jnp.where(iota((16, 128), 1) < 64, placed[0:16], placed[16:32]).astype(BF16)
    for j in range(8):
        out_ref[j, :, 0:2048] = x_ref[0]
        out_ref[j, :, 2048:2176] = packed


def frame_rows_kernel(gathered_ref, out_ref):
    low, high = (
        sum(gathered_ref[4 * half + i, :, 2048:2176].astype(F32) for i in range(4)) for half in range(2)
    )
    plain = lax.axis_index("core") == 0
    low, high = jnp.where(plain, low, high), jnp.where(plain, high, low)
    left = iota((16, 128), 1) < 64
    first = jnp.where(left, low, pltpu.roll(high, 64, 1))
    second = jnp.where(left, pltpu.roll(low, 64, 1), high)
    out_ref[:, 0, :] = jnp.concatenate([first, second, first, second], axis=0)


def modulation(rows_ref):
    values = jnp.concatenate([rows_ref[0:32, 0, :], rows_ref[32:64, 0, :]], axis=1).astype(BF16)
    n = iota((256, 256), 1)
    source = ((n >> 2) & 1) * 128 + ((n >> 3) & 7) * 16 + (n >> 6) * 4 + (n & 3)
    permute = jnp.where(iota((256, 256), 0) == source, 1.0, 0.0).astype(BF16)
    ordered = dot(values, permute).astype(BF16)
    own_block = (iota((32, 2048), 1) >> 6) == iota((32, 2048), 0)
    rows = []
    for k in range(4):
        lane = (iota((128, 2048), 1) & 63) + 64 * (k % 2)
        spread = jnp.where(iota((128, 2048), 0) == lane, 1.0, 0.0).astype(BF16)
        part = ordered[:, 128 * (k // 2) : 128 * (k // 2) + 128]
        wide = jnp.where(own_block, dot(part, spread), 0.0)
        rows.append(jnp.sum(wide, axis=0, keepdims=True))
    return rows


def normed_rows(rows, scale, shift):
    v = rows.astype(F32)
    centre = v - jnp.mean(v, axis=-1, keepdims=True)
    spread = jnp.mean(centre * centre, axis=-1, keepdims=True)
    return (centre * lax.rsqrt(spread + 1e-05) * (1.0 + scale) + shift).astype(BF16)


def unit(v):
    return v * lax.rsqrt(jnp.mean(v * v, axis=-1, keepdims=True) + 1e-06)


def plane_project_kernel(
    gathered_ref, rows_ref, own_ref, other_ref, other_any, q_ref, kv_ref, mod_ref, normed_ref, last_ref, sem
):
    copy = pltpu.make_async_copy(other_any.at[2], last_ref, sem)
    copy.start()
    rows = modulation(rows_ref)
    for k in range(4):
        mod_ref[k : k + 1, :] = rows[k]
    for j in range(8):
        normed_ref[16 * j : 16 * j + 16, :] = normed_rows(gathered_ref[j, :, 0:2048], rows[0], rows[1])
    normed = normed_ref[...]
    even = lax.axis_index("zl") == 0
    for i in range(3):
        if i == 2:
            copy.wait()
        both = dot(normed, jnp.concatenate([own_ref[i], last_ref[...] if i == 2 else other_ref[i]], axis=1))
        own, other = both[:, 0:128], both[:, 128:256]
        if i < 2:
            own, other = unit(own), unit(other)
        for h in range(2):
            part = jnp.where(even, own, other) if h == 0 else jnp.where(even, other, own)
            if i == 0:
                q_ref[h] = part.astype(BF16)
            else:
                kv_ref[h, :, 128 * (i - 1) : 128 * i] = part.astype(BF16)


def plane_attend_kernel(scale_ref, q_ref, kv_ref, own_ref, other_ref, out_ref):
    even = lax.axis_index("zl") == 0
    y = lax.axis_index("y")
    heads = []
    for h in range(2):
        scale = scale_ref[0, 2 * y + h] / 128.0
        keys = jnp.concatenate([kv_ref[0, h, :, 0:128], kv_ref[1, h, :, 0:128]], axis=0)
        values = jnp.concatenate([kv_ref[0, h, :, 128:256], kv_ref[1, h, :, 128:256]], axis=0)
        scores = dot(q_ref[h], keys, ((1,), (1,))) * scale
        expo = jnp.exp(scores - jnp.max(scores, axis=-1, keepdims=True))
        weights = (expo / jnp.sum(expo, axis=-1, keepdims=True)).astype(BF16)
        heads.append(dot(weights, values))
    own = jnp.where(even, heads[0], heads[1])
    other = jnp.where(even, heads[1], heads[0])
    attended = jnp.concatenate([own, other], axis=1).astype(BF16)
    mixing = jnp.concatenate([own_ref[0], other_ref[0]], axis=0)
    for c in range(0, 2048, 512):
        part = dot(attended, mixing[:, c : c + 512]).astype(BF16)
        for j in range(8):
            out_ref[j, :, c : c + 512] = part[16 * j : 16 * j + 16]


def hold_kernel(weight_ref, out_ref):
    out_ref[...] = weight_ref[...]


def hold(weight):
    block = (2,) + weight.shape[1:]
    return pl.pallas_call(
        hold_kernel,
        grid=(1,),
        out_shape=jax.ShapeDtypeStruct(block, weight.dtype),
        in_specs=[pl.BlockSpec(block, lambda i: (0, 0, 0))],
        out_specs=pl.BlockSpec(block, lambda i: (0, 0, 0)),
        compiler_params=pltpu.CompilerParams(vmem_limit_bytes=VMEM_LIMIT),
        cost_estimate=pl.CostEstimate(flops=0, bytes_accessed=2**22, transcendentals=0),
    )(weight)


def mix_kernel(terms_ref, x_ref, mixed_ref, spread_ref):
    total = terms_ref[0].astype(F32)
    for j in range(1, 8):
        total = total + terms_ref[j].astype(F32)
    mixed = (x_ref[0].astype(F32) + total).astype(BF16)
    mixed_ref[0] = mixed
    for j in range(8):
        spread_ref[j] = mixed


def clock_project_kernel(gathered_ref, mod_ref, own_ref, other_ref, out_ref, normed_ref):
    scale, shift = mod_ref[2:3, :], mod_ref[3:4, :]
    for j in range(8):
        normed_ref[16 * j : 16 * j + 16, :] = normed_rows(gathered_ref[j], scale, shift)
    normed = normed_ref[...]
    even = lax.axis_index("zl") == 0
    plain = lax.axis_index("core") == 0
    upper = iota((16, 8, 128), 1) < 4
    for i in range(3):
        both = dot(normed, jnp.concatenate([own_ref[i], other_ref[i]], axis=1))
        own, other = both[:, 0:128], both[:, 128:256]
        if i < 2:
            own, other = unit(own), unit(other)
        first = jnp.where(even, own, other).reshape(16, 8, 128)
        second = jnp.where(even, other, own).reshape(16, 8, 128)
        low = jnp.where(upper, first, pltpu.roll(second, 4, 1))
        high = jnp.where(upper, pltpu.roll(first, 4, 1), second)
        rows = jnp.stack([low, high], axis=1).reshape(256, 128).astype(BF16)
        halves = rows[0:128], rows[128:256]
        out_ref[0:128, 128 * i : 128 * i + 128] = jnp.where(plain, halves[0], halves[1])
        out_ref[128:256, 128 * i : 128 * i + 128] = jnp.where(plain, halves[1], halves[0])


def frame_of(index):
    return (index & 24) + (index & 3) * 2 + ((index >> 2) & 1)


def clock_attend_kernel(scale_ref, rows_ref, out_ref):
    y = lax.axis_index("y")
    queries, keys, values = rows_ref[:, 0:128], rows_ref[:, 128:256], rows_ref[:, 256:384]
    r, c = iota((256, 256), 0), iota((256, 256), 1)
    seen = ((r & 7) == (c & 7)) & (frame_of(c >> 3) <= frame_of(r >> 3))
    scale = jnp.where(
        (iota((256, 1), 0) & 7) < 4, scale_ref[1, 2 * y] / 128.0, scale_ref[1, 2 * y + 1] / 128.0
    )
    scores = jnp.where(seen, dot(queries, keys, ((1,), (1,))) * scale, -1e30)
    expo = jnp.exp(scores - jnp.max(scores, axis=-1, keepdims=True))
    weights = (expo / jnp.sum(expo, axis=-1, keepdims=True)).astype(BF16)
    moved = dot(weights, values).reshape(8, 2, 2, 8, 128)
    upper = iota((8, 2, 8, 128), 2) < 4
    even, odd = moved[:, :, 0], moved[:, :, 1]
    first = jnp.where(upper, even, pltpu.roll(odd, 4, 2))
    second = jnp.where(upper, pltpu.roll(even, 4, 2), odd)
    out_ref[...] = jnp.stack([first, second], axis=1).reshape(256, 128).astype(BF16)


def body(x, grades, table, plane_weight, mixing, clock_weight, stretch):
    def shape(*dims, dtype=BF16):
        return jax.ShapeDtypeStruct(dims, dtype)

    def trade(value, axes, groups=None):
        return lax.all_to_all(
            value, axes, split_axis=0, concat_axis=0, tiled=True, axis_index_groups=groups
        )

    ring = [list(range(8)), [8 + (y + 4) % 8 for y in range(8)]]

    def trade_ring(value):
        return trade(value, ("core", "y"), ring)

    swaps = []
    for z in range(8):
        for core in range(2):
            z_to = (z ^ 1) if core == 0 else (z + 1 if z % 2 else z - 1) % 8
            swaps.append(((z // 2 * 2 + core) * 2 + z % 2, (z_to // 2 * 2 + core) * 2 + z_to % 2))

    project_scratch = [
        pltpu.VMEM((128, 2048), BF16),
        pltpu.VMEM((2048, 128), BF16),
        pltpu.SemaphoreType.DMA,
    ]

    def other_head(weight):
        return lax.ppermute(weight, ("zh", "core", "zl"), swaps)

    plane_weight = jnp.transpose(plane_weight, (1, 2, 0, 3)).reshape(3, 2048, 128)
    clock_weight = jnp.transpose(clock_weight, (1, 2, 0, 3)).reshape(3, 2048, 128)
    packed = call(
        pack_kernel, shape(8, 16, 2176), grades.reshape(1, -1), jnp.transpose(table, (1, 2, 0)), x
    )
    far_plane = other_head(plane_weight)
    packed, mixing = lax.optimization_barrier((packed, mixing))
    far_mixing = other_head(mixing)
    gathered = trade_ring(packed)
    own_rows = call(frame_rows_kernel, shape(64, 1, 128, dtype=F32), gathered)
    rows = trade(own_rows, ("zl",) + TM)
    queries, kv, mod = call(
        plane_project_kernel,
        (shape(2, 128, 128), shape(2, 128, 256), shape(8, 2048, dtype=F32)),
        gathered,
        rows,
        plane_weight,
        hold(far_plane),
        far_plane,
        anywhere=(4,),
        flops=2 * 128 * 2048 * 768,
        scratch=project_scratch,
    )
    terms = call(
        plane_attend_kernel,
        shape(8, 16, 2048),
        stretch,
        queries,
        lax.all_gather(kv, "zl"),
        mixing,
        far_mixing,
        in_smem=(0,),
        flops=2 * 128 * 2048 * 256,
    )
    clock_weight, terms = lax.optimization_barrier((clock_weight, terms))
    far_clock = other_head(clock_weight)
    mixed, spread = call(mix_kernel, (shape(1, 16, 2048), shape(8, 16, 2048)), trade_ring(terms), x)
    spread, far_clock = lax.optimization_barrier((spread, far_clock))
    clock_rows = call(
        clock_project_kernel,
        shape(256, 384),
        trade_ring(spread),
        mod,
        clock_weight,
        far_clock,
        flops=2 * 128 * 2048 * 768,
        scratch=[pltpu.VMEM((128, 2048), BF16)],
    )
    by_position = trade(clock_rows, ("zh", "core", "x"))
    moved = call(clock_attend_kernel, shape(256, 128), stretch, by_position, in_smem=(0,))
    heads = trade(moved, ("zh", "core", "zl", "x"))
    return mixed, heads.reshape(1, 256, 128)


def solution(mesh):
    named = Mesh(mesh.devices.reshape(4, 4, 2, 8, 2), ("zh", "x", "core", "y", "zl"))
    space = ("y", "zl")
    return jax.shard_map(
        body,
        mesh=named,
        in_specs=(
            P(TM, space, None),
            P(),
            P(None, None, TM + space),
            P(None, None, space, None),
            P(space, None, None),
            P(None, None, space, None),
            P(),
        ),
        out_specs=(P(TM, space, None), P(TM, None, space)),
        check_vma=False,
    )
```
